32 devices in a mesh: groups: 2 (over x), context: 8 (over z, y), tensor: 2 (over core).
Axes of the slice: x: 2, y: 2, z: 4, core: 2. Of those that a mesh axis runs over, the one named last changes fastest.
Arguments:
- queries: bfloat16 [8192, 2048], P(('groups', 'context'), 'tensor'), parts along dimension 0, may hold values from -60 to 60
- keys: bfloat16 [8192, 1024], P(('groups', 'context'), 'tensor'), parts along dimension 0, may hold values from -6 to 6
- values: bfloat16 [8192, 1024], P(('groups', 'context'), 'tensor'), parts along dimension 0, may hold values from -6 to 6
Outputs:
- attended: bfloat16 [8192, 2048], P(('groups', 'context', 'tensor')), parts along dimension 0
The draws below stay inside these ranges and needn't reach their ends.
There are 2 independent parts, one for each index of `groups`. The reference program is written for one: setup_inputs(seed, part) draws one part's arguments, and reference() takes and returns one part's arrays. A program takes and returns all parts, laid end to end along the dimension named above; each array names one. Nothing has to cross between parts.
All inputs are finite; a program needn't handle non-finite values.
Results may differ from the reference program's by a relative error of at most 0.0049.
Values may be sent and summed in bfloat16 or wider, within the bound.
A program may use at most 64 MiB of HBM per device.

```python
import math
import jax
import jax.numpy as jnp
from jax import lax

HEADS = 16
KV_HEADS = 8
HEAD_DIM = 128
WINDOW = 2048
TOKENS = 4096


def draw_queries(key, part):
    scale_key = jax.random.fold_in(key, 11)
    entry_key = jax.random.fold_in(key, 12)
    head_scales = jnp.exp(jax.random.uniform(scale_key, (HEADS,), jnp.float32, jnp.log(0.3), jnp.log(10.0)))
    column_scales = jnp.repeat(head_scales, HEAD_DIM)
    entries = jnp.clip(jax.random.normal(entry_key, (TOKENS, HEADS * HEAD_DIM), jnp.float32), -6.0, 6.0)
    return (entries * column_scales[None, :]).astype(jnp.bfloat16)


def block_scale(key, shape, split, smallest, top_value):
    loudness, own = 1.0, jax.random.fold_in(key, 6)
    for axis_at, blocks in split:
        heights = jnp.exp(jax.random.uniform(jax.random.fold_in(own, axis_at), (blocks,), jnp.float32, smallest / len(split), top_value / len(split)))
        loudness = loudness * jnp.repeat(heights, shape[axis_at] // blocks).reshape([-1 if axis == axis_at else 1 for axis in range(len(shape))])
    return loudness


def bell_draw(own_key, extent, scale, reach, pieces=(), kind=jnp.bfloat16):
    result = scale * jax.random.normal(own_key, extent, jnp.float32)
    if pieces:
        result = result * block_scale(own_key, extent, pieces, -0.22, 0.18)
    return jnp.clip(result, -reach, reach).astype(kind)


def setup_inputs(seed: int = 0, part: int = 0) -> dict:
    key_list = jax.random.split(jax.random.key(seed), 4)
    part_splits = jax.random.split(jax.random.fold_in(key_list[3], part), 4)
    return {
        "queries": draw_queries(jax.random.fold_in(jax.random.fold_in(key_list[3], part), 71), part),
        "keys": bell_draw(part_splits[1], (TOKENS, KV_HEADS * HEAD_DIM), 1.0, 6.0, ((0, 8), (1, 2))),
        "values": bell_draw(part_splits[2], (TOKENS, KV_HEADS * HEAD_DIM), 1.0, 6.0, ((0, 8), (1, 2))),
    }


cap_value = 50.0
query_scale = 144.0 ** -0.5


def reference(queries, keys, values):
    tokens = queries.shape[0]
    group_size = HEADS // KV_HEADS
    row_block = math.gcd(512, tokens)
    key_span = WINDOW + row_block
    pad_keys = jnp.concatenate([jnp.zeros((WINDOW, keys.shape[1]), keys.dtype), keys], axis=0)
    pad_values = jnp.concatenate([jnp.zeros((WINDOW, values.shape[1]), values.dtype), values], axis=0)
    query_heads = queries.reshape(tokens, HEADS, HEAD_DIM)

    def attend_block(start_row):
        query_rows = lax.dynamic_slice_in_dim(query_heads, start_row, row_block, 0).astype(jnp.float32)
        key_rows = lax.dynamic_slice_in_dim(pad_keys, start_row, key_span, 0).astype(jnp.float32)
        key_rows = jnp.repeat(key_rows.reshape(key_span, KV_HEADS, HEAD_DIM), group_size, axis=1)
        value_rows = lax.dynamic_slice_in_dim(pad_values, start_row, key_span, 0).astype(jnp.float32)
        value_rows = jnp.repeat(value_rows.reshape(key_span, KV_HEADS, HEAD_DIM), group_size, axis=1)
        scores = jnp.einsum("ihd,jhd->hij", query_rows, key_rows) * query_scale
        capped = cap_value * jnp.tanh(scores / cap_value)
        query_pos = start_row + jnp.arange(row_block, dtype=jnp.int32)
        key_pos = start_row - WINDOW + jnp.arange(key_span, dtype=jnp.int32)
        allowed = (key_pos[None, :] <= query_pos[:, None]) & (key_pos[None, :] > query_pos[:, None] - WINDOW) & (key_pos[None, :] >= 0)
        exp_terms = jnp.where(allowed[None], jnp.exp(capped), jnp.zeros_like(capped))
        totals = jnp.sum(exp_terms, axis=-1)
        rounded = lax.optimization_barrier(exp_terms.astype(jnp.bfloat16)).astype(jnp.float32)
        weighted = jnp.einsum("hij,jhd->ihd", rounded, value_rows)
        mixed = weighted / jnp.transpose(totals)[:, :, None]
        return mixed.astype(jnp.bfloat16).reshape(row_block, HEADS * HEAD_DIM)

    starts = jnp.arange(0, tokens, row_block, dtype=jnp.int32)
    return lax.map(attend_block, starts).reshape(tokens, HEADS * HEAD_DIM)
```

```python
import functools
import math

import jax
import jax.numpy as jnp
from jax import lax
from jax.experimental import pallas as pl
from jax.experimental.pallas import tpu as pltpu
from jax.sharding import PartitionSpec as P

HEAD_DIM = 128
WINDOW = 2048
SPAN = 4
MESH = pl.DeviceIdType.MESH

CAP = 50.0
SCORE_FACTOR = 144.0 ** (-0.5) / CAP
EXP_FACTOR = CAP * math.log2(math.e)


def kernel(
    blocks,
    q_ref,
    k_ref,
    v_ref,
    out_ref,
    held,
    acc,
    outgoing,
    up_own_send,
    up_relay_send,
    cross_send,
    recv_sem,
    out_send,
    out_recv,
):
    rows = q_ref.shape[0]
    half = rows // 2
    kv_heads = k_ref.shape[1] // HEAD_DIM
    own_cols = q_ref.shape[1]
    c = lax.axis_index("context")
    t = lax.axis_index("tensor")
    odd = lax.rem(c, 2)
    pair = c + 1 - 2 * odd
    other = 1 - t
    has_up = c + 2 < blocks
    has_down = c >= 2

    barrier = pltpu.get_barrier_semaphore()
    pl.semaphore_signal(barrier, inc=1, device_id={"context": pair}, device_id_type=MESH)
    pl.semaphore_signal(barrier, inc=1, device_id={"tensor": other}, device_id_type=MESH)

    @pl.when(has_up)
    def _():
        pl.semaphore_signal(barrier, inc=1, device_id={"context": c + 2}, device_id_type=MESH)

    @pl.when(has_down)
    def _():
        pl.semaphore_signal(barrier, inc=1, device_id={"context": c - 2}, device_id_type=MESH)

    pl.semaphore_wait(barrier, 2 + has_up.astype(jnp.int32) + has_down.astype(jnp.int32))

    def columns(head):
        return pl.ds(pl.multiple_of(head * HEAD_DIM, HEAD_DIM), HEAD_DIM)

    def source(slot, which, h):
        if slot == 0:
            return (k_ref, v_ref)[which].at[:, columns(h)]
        return held.at[slot - 1, which, h]

    def copy(slot, into, which, h, to, send):
        return pltpu.make_async_remote_copy(
            src_ref=source(slot, which, h),
            dst_ref=held.at[into - 1, which, h],
            send_sem=send,
            recv_sem=recv_sem.at[into - 1, which, h],
            device_id={"context": to},
            device_id_type=MESH,
        )

    def up_own(which, h):
        return copy(0, 2, which, h, c + 2, up_own_send.at[which, h])

    def up_relay(which, h):
        return copy(2, 4, which, h, c + 2, up_relay_send.at[which, h])

    def cross(slot, into, which, h):
        return copy(slot, into, which, h, pair, cross_send.at[(into - 1) // 2, which, h])

    @pl.loop(0, kv_heads)
    def _(h):
        for which in range(2):

            @pl.when(has_up)
            def _():
                up_own(which, h).start()

            @pl.when(odd == 0)
            def _():
                cross(0, 1, which, h).start()

    def landed(slot, which, h):
        copy(0, slot, which, h, pair, cross_send.at[0, which, h]).wait_recv()

    def terms(h, g, row_at, row_count, slot, key_at, key_count, mask):
        q = q_ref[pl.ds(row_at, row_count), columns(2 * h + g)]
        key_rows = source(slot, 0, h)[pl.ds(key_at, key_count), :]
        value_rows = source(slot, 1, h)[pl.ds(key_at, key_count), :]
        scores = lax.dot_general(
            q, key_rows, (((1,), (1,)), ((), ())), preferred_element_type=jnp.float32
        )
        exp_terms = jnp.exp2(EXP_FACTOR * jnp.tanh(scores * SCORE_FACTOR))
        if mask is not None:
            i = row_at + lax.broadcasted_iota(jnp.int32, exp_terms.shape, 0)
            j = key_at + lax.broadcasted_iota(jnp.int32, exp_terms.shape, 1)
            allowed = j <= i if mask == "own" else j > i
            exp_terms = jnp.where(allowed, exp_terms, jnp.zeros_like(exp_terms))
        beside = jnp.concatenate([value_rows, jnp.ones_like(value_rows)], axis=1)
        return jnp.dot(
            exp_terms.astype(jnp.bfloat16), beside, preferred_element_type=jnp.float32
        )

    def attend_own(h):
        @pl.loop(0, 2)
        def _(g):
            acc[2 * h + g, pl.ds(0, half), :] = terms(h, g, 0, half, 0, 0, half, "own")
            acc[2 * h + g, pl.ds(half, half), :] = terms(h, g, half, half, 0, 0, rows, "own")

    def attend_far(h):
        @pl.loop(0, 2)
        def _(g):
            acc[2 * h + g, pl.ds(0, half), :] += terms(h, g, 0, half, 4, 0, rows, "far")
            acc[2 * h + g, pl.ds(half, half), :] += terms(h, g, half, half, 4, half, half, "far")

    def attend_whole(h, slot):
        @pl.loop(0, 4)
        def _(step):
            g = step // 2
            row_at = pl.multiple_of(lax.rem(step, 2) * half, half)
            acc[2 * h + g, pl.ds(row_at, half), :] += terms(
                h, g, row_at, half, slot, 0, rows, None
            )

    def take_two(h):
        @pl.when(has_down)
        def _():
            for which in range(2):
                landed(2, which, h)

                @pl.when(has_up)
                def _():
                    up_relay(which, h).start()

                @pl.when(odd == 0)
                def _():
                    cross(2, 3, which, h).start()

                @pl.when(odd == 1)
                def _():
                    cross(2, 1, which, h).start()

            attend_whole(h, 2)

    def take_one(h):
        @pl.when(c >= 1)
        def _():
            for which in range(2):
                landed(1, which, h)
            attend_whole(h, 1)

    def take_four(h):
        @pl.when(c >= 4)
        def _():
            for which in range(2):
                landed(4, which, h)

                @pl.when(odd == 1)
                def _():
                    cross(4, 3, which, h).start()

            attend_far(h)

    def hand_over(h):
        col = pl.multiple_of(t * own_cols + h * 2 * HEAD_DIM, 2 * HEAD_DIM)
        return pltpu.make_async_remote_copy(
            src_ref=outgoing.at[h],
            dst_ref=out_ref.at[:, pl.ds(col, 2 * HEAD_DIM)],
            send_sem=out_send.at[h],
            recv_sem=out_recv.at[h],
            device_id={"tensor": other},
            device_id_type=MESH,
        )

    def take_three(h):
        @pl.when(c >= 3)
        def _():
            for which in range(2):
                landed(3, which, h)
            attend_whole(h, 3)

        def finished(g, owner):
            part = acc[2 * h + g, pl.ds(pl.multiple_of(owner * half, half), half), :]
            return (part[:, :HEAD_DIM] / part[:, HEAD_DIM:]).astype(out_ref.dtype)

        for g in range(2):
            outgoing[h, :, pl.ds(g * HEAD_DIM, HEAD_DIM)] = finished(g, other)
        hand_over(h).start()
        for g in range(2):
            col = pl.multiple_of(t * own_cols + (2 * h + g) * HEAD_DIM, HEAD_DIM)
            out_ref[:, pl.ds(col, HEAD_DIM)] = finished(g, t)

    last = kv_heads - 1

    @pl.loop(0, kv_heads)
    def _(h):
        attend_own(h)

    take_two(0)

    @pl.loop(0, last)
    def _(h):
        take_two(h + 1)
        take_one(h)

    take_four(0)
    take_one(last)

    @pl.loop(0, last)
    def _(h):
        take_four(h + 1)
        take_three(h)

    take_three(last)

    @pl.loop(0, kv_heads)
    def _(h):
        hand_over(h).wait()
        for which in range(2):

            @pl.when(has_up)
            def _():
                up_own(which, h).wait_send()

            @pl.when(has_up & has_down)
            def _():
                up_relay(which, h).wait_send()

            @pl.when((odd == 0) | (c >= 2))
            def _():
                cross(0, 1, which, h).wait_send()

            @pl.when(((odd == 0) & (c >= 2)) | (c >= 4))
            def _():
                cross(0, 3, which, h).wait_send()


def local(blocks, queries, keys, values):
    rows = queries.shape[0]
    kv_heads = keys.shape[1] // HEAD_DIM
    heads = queries.shape[1] // HEAD_DIM
    assert WINDOW == SPAN * rows and blocks % 2 == 0 and heads == 2 * kv_heads
    return pl.pallas_call(
        functools.partial(kernel, blocks),
        out_shape=jax.ShapeDtypeStruct((rows // 2, 2 * queries.shape[1]), queries.dtype),
        in_specs=[pl.BlockSpec(memory_space=pltpu.VMEM)] * 3,
        out_specs=pl.BlockSpec(memory_space=pltpu.VMEM),
        scratch_shapes=[
            pltpu.VMEM((SPAN, 2, kv_heads, rows, HEAD_DIM), keys.dtype),
            pltpu.VMEM((heads, rows, 2 * HEAD_DIM), jnp.float32),
            pltpu.VMEM((kv_heads, rows // 2, 2 * HEAD_DIM), queries.dtype),
            pltpu.SemaphoreType.DMA((2, kv_heads)),
            pltpu.SemaphoreType.DMA((2, kv_heads)),
            pltpu.SemaphoreType.DMA((2, 2, kv_heads)),
            pltpu.SemaphoreType.DMA((SPAN, 2, kv_heads)),
            pltpu.SemaphoreType.DMA((kv_heads,)),
            pltpu.SemaphoreType.DMA((kv_heads,)),
        ],
        compiler_params=pltpu.CompilerParams(
            collective_id=0, has_side_effects=True, vmem_limit_bytes=40 * 1024 * 1024
        ),
    )(queries, keys, values)


def solution(mesh):
    return jax.shard_map(
        functools.partial(local, mesh.shape["context"]),
        mesh=mesh,
        in_specs=(P(("groups", "context"), "tensor"),) * 3,
        out_specs=P(("groups", "context", "tensor"), None),
        check_vma=False,
    )
```

```python
import functools
import math

import jax
import jax.numpy as jnp
from jax import lax
from jax.experimental import pallas as pl
from jax.experimental.pallas import tpu as pltpu
from jax.sharding import PartitionSpec as P

HEAD_DIM = 128
WINDOW = 2048
SPAN = 4
MESH = pl.DeviceIdType.MESH

CAP = 50.0
SCORE_FACTOR = 144.0 ** (-0.5) / CAP
EXP_FACTOR = CAP * math.log2(math.e)


def kernel(
    blocks,
    q_hbm,
    k_hbm,
    v_hbm,
    out_ref,
    q_ref,
    k_ref,
    v_ref,
    held,
    acc,
    outgoing,
    kept,
    up_own_send,
    up_relay_send,
    cross_send,
    recv_sem,
    out_send,
    out_recv,
    fetch_sem,
    keep_sem,
):
    rows = q_ref.shape[0]
    half = rows // 2
    kv_heads = k_ref.shape[1] // HEAD_DIM
    own_cols = q_ref.shape[1]
    c = lax.axis_index("context")
    t = lax.axis_index("tensor")
    odd = lax.rem(c, 2)
    pair = c + 1 - 2 * odd
    other = 1 - t
    has_up = c + 2 < blocks
    has_down = c >= 2

    fetches = [
        pltpu.make_async_copy(far, near, fetch_sem.at[at])
        for at, (far, near) in enumerate(((q_hbm, q_ref), (k_hbm, k_ref), (v_hbm, v_ref)))
    ]
    for fetch in fetches:
        fetch.start()

    barrier = pltpu.get_barrier_semaphore()
    pl.semaphore_signal(barrier, inc=1, device_id={"context": pair}, device_id_type=MESH)
    pl.semaphore_signal(barrier, inc=1, device_id={"tensor": other}, device_id_type=MESH)

    @pl.when(has_up)
    def _():
        pl.semaphore_signal(barrier, inc=1, device_id={"context": c + 2}, device_id_type=MESH)

    @pl.when(has_down)
    def _():
        pl.semaphore_signal(barrier, inc=1, device_id={"context": c - 2}, device_id_type=MESH)

    pl.semaphore_wait(barrier, 2 + has_up.astype(jnp.int32) + has_down.astype(jnp.int32))

    def columns(head):
        return pl.ds(pl.multiple_of(head * HEAD_DIM, HEAD_DIM), HEAD_DIM)

    def source(slot, which, h):
        if slot == 0:
            return (k_ref, v_ref)[which].at[:, columns(h)]
        return held.at[slot - 1, which, h]

    def copy(slot, into, which, h, to, send):
        return pltpu.make_async_remote_copy(
            src_ref=(
                (k_hbm, v_hbm)[which].at[:, columns(h)]
                if slot == 0
                else held.at[slot - 1, which, h]
            ),
            dst_ref=held.at[into - 1, which, h],
            send_sem=send,
            recv_sem=recv_sem.at[into - 1, which, h],
            device_id={"context": to},
            device_id_type=MESH,
        )

    def up_own(which, h):
        return copy(0, 2, which, h, c + 2, up_own_send.at[which, h])

    def up_relay(which, h):
        return copy(2, 4, which, h, c + 2, up_relay_send.at[which, h])

    def cross(slot, into, which, h):
        return copy(slot, into, which, h, pair, cross_send.at[(into - 1) // 2, which, h])

    def landed(slot, which, h):
        copy(0, slot, which, h, pair, cross_send.at[0, which, h]).wait_recv()

    def terms(h, g, row_at, row_count, slot, key_at, key_count, mask):
        q = q_ref[pl.ds(row_at, row_count), columns(2 * h + g)]
        key_rows = source(slot, 0, h)[pl.ds(key_at, key_count), :]
        value_rows = source(slot, 1, h)[pl.ds(key_at, key_count), :]
        scores = lax.dot_general(
            q, key_rows, (((1,), (1,)), ((), ())), preferred_element_type=jnp.float32
        )
        exp_terms = jnp.exp2(EXP_FACTOR * jnp.tanh(scores * SCORE_FACTOR))
        if mask is not None:
            i = row_at + lax.broadcasted_iota(jnp.int32, exp_terms.shape, 0)
            j = key_at + lax.broadcasted_iota(jnp.int32, exp_terms.shape, 1)
            allowed = j <= i if mask == "own" else j > i
            exp_terms = jnp.where(allowed, exp_terms, jnp.zeros_like(exp_terms))
        beside = jnp.concatenate([value_rows, jnp.ones_like(value_rows)], axis=1)
        return jnp.dot(
            exp_terms.astype(jnp.bfloat16), beside, preferred_element_type=jnp.float32
        )

    def attend_own(h):
        @pl.loop(0, 2)
        def _(g):
            acc[2 * h + g, pl.ds(0, half), :] = terms(h, g, 0, half, 0, 0, half, "own")
            acc[2 * h + g, pl.ds(half, half), :] = terms(h, g, half, half, 0, 0, rows, "own")

    def attend_far(h):
        @pl.loop(0, 2)
        def _(g):
            acc[2 * h + g, pl.ds(0, half), :] += terms(h, g, 0, half, 4, 0, rows, "far")
            acc[2 * h + g, pl.ds(half, half), :] += terms(h, g, half, half, 4, half, half, "far")

    def attend_whole(h, slot):
        @pl.loop(0, 4)
        def _(step):
            g = step // 2
            row_at = pl.multiple_of(lax.rem(step, 2) * half, half)
            acc[2 * h + g, pl.ds(row_at, half), :] += terms(
                h, g, row_at, half, slot, 0, rows, None
            )

    def send_own(h, which):
        @pl.when(has_up)
        def _():
            up_own(which, h).start()

        @pl.when(odd == 0)
        def _():
            cross(0, 1, which, h).start()

    def sent_own(h, which):
        @pl.when(has_up)
        def _():
            up_own(which, h).wait_send()

        @pl.when(odd == 0)
        def _():
            cross(0, 1, which, h).wait_send()

    def send_relay(h, which):
        @pl.when(has_up & has_down)
        def _():
            up_relay(which, h).start()

        @pl.when((odd == 0) & has_down)
        def _():
            cross(2, 3, which, h).start()

    def sent_relay(h, which):
        @pl.when(has_up & has_down)
        def _():
            up_relay(which, h).wait_send()

        @pl.when((odd == 0) & has_down)
        def _():
            cross(2, 3, which, h).wait_send()

    def take(slot, h, which):
        @pl.when(c >= slot)
        def _():
            landed(slot, which, h)

            @pl.when(odd == 1)
            def _():
                cross(slot, slot - 1, which, h).start()

    def attend(slot, h):
        @pl.when(c >= slot)
        def _():
            if slot % 2 == 1:
                for which in range(2):
                    landed(slot, which, h)
            if slot == 4:
                attend_far(h)
            else:
                attend_whole(h, slot)

    def out_columns(h):
        col = pl.multiple_of(t * own_cols + h * 2 * HEAD_DIM, 2 * HEAD_DIM)
        return out_ref.at[:, pl.ds(col, 2 * HEAD_DIM)]

    def keep(h):
        return pltpu.make_async_copy(kept.at[h], out_columns(h), keep_sem.at[h])

    def hand_over(h):
        return pltpu.make_async_remote_copy(
            src_ref=outgoing.at[h],
            dst_ref=out_columns(h),
            send_sem=out_send.at[h],
            recv_sem=out_recv.at[h],
            device_id={"tensor": other},
            device_id_type=MESH,
        )

    def finish(h):
        attend(3, h)

        def finished(g, owner):
            part = acc[2 * h + g, pl.ds(pl.multiple_of(owner * half, half), half), :]
            return (part[:, :HEAD_DIM] / part[:, HEAD_DIM:]).astype(out_ref.dtype)

        for g in range(2):
            outgoing[h, :, pl.ds(g * HEAD_DIM, HEAD_DIM)] = finished(g, other)
        hand_over(h).start()
        for g in range(2):
            kept[h, :, pl.ds(g * HEAD_DIM, HEAD_DIM)] = finished(g, t)
        keep(h).start()

    last = kv_heads - 1
    for which in range(2):
        send_own(0, which)
    for fetch in fetches:
        fetch.wait()
    attend_own(0)

    @pl.loop(1, kv_heads)
    def _(h):
        sent_own(h - 1, 0)
        send_own(h, 0)
        take(2, h - 1, 0)
        attend_own(h)
        sent_own(h - 1, 1)
        send_own(h, 1)
        take(2, h - 1, 1)
        attend(2, h - 1)

        @pl.when(h >= 2)
        def _():
            attend(1, h - 2)

    for which in range(2):
        sent_own(last, which)
        send_relay(0, which)
        take(2, last, which)
        if which == 0:
            attend(1, last - 1)
    attend(2, last)

    for which in range(2):
        sent_relay(0, which)
        send_relay(1, which)
        take(4, 0, which)
        if which == 0:
            attend(1, last)
    attend(4, 0)

    @pl.loop(2, kv_heads)
    def _(h):
        sent_relay(h - 1, 0)
        send_relay(h, 0)
        take(4, h - 1, 0)
        finish(h - 2)
        sent_relay(h - 1, 1)
        send_relay(h, 1)
        take(4, h - 1, 1)
        attend(4, h - 1)

    take(4, last, 0)
    finish(last - 1)
    take(4, last, 1)
    attend(4, last)
    finish(last)
    for which in range(2):
        sent_relay(last, which)

    @pl.loop(0, kv_heads)
    def _(h):
        keep(h).wait()
        hand_over(h).wait()
        for which in range(2):

            @pl.when((odd == 1) & (c >= 2))
            def _():
                cross(2, 1, which, h).wait_send()

            @pl.when((odd == 1) & (c >= 4))
            def _():
                cross(4, 3, which, h).wait_send()


def local(blocks, queries, keys, values):
    rows = queries.shape[0]
    kv_heads = keys.shape[1] // HEAD_DIM
    heads = queries.shape[1] // HEAD_DIM
    assert WINDOW == SPAN * rows and blocks % 2 == 0 and heads == 2 * kv_heads
    return pl.pallas_call(
        functools.partial(kernel, blocks),
        out_shape=jax.ShapeDtypeStruct((rows // 2, 2 * queries.shape[1]), queries.dtype),
        in_specs=[pl.BlockSpec(memory_space=pltpu.HBM)] * 3,
        out_specs=pl.BlockSpec(memory_space=pltpu.HBM),
        scratch_shapes=[
            pltpu.VMEM(queries.shape, queries.dtype),
            pltpu.VMEM(keys.shape, keys.dtype),
            pltpu.VMEM(values.shape, values.dtype),
            pltpu.VMEM((SPAN, 2, kv_heads, rows, HEAD_DIM), keys.dtype),
            pltpu.VMEM((heads, rows, 2 * HEAD_DIM), jnp.float32),
            pltpu.VMEM((kv_heads, rows // 2, 2 * HEAD_DIM), queries.dtype),
            pltpu.VMEM((kv_heads, rows // 2, 2 * HEAD_DIM), queries.dtype),
            pltpu.SemaphoreType.DMA((2, kv_heads)),
            pltpu.SemaphoreType.DMA((2, kv_heads)),
            pltpu.SemaphoreType.DMA((2, 2, kv_heads)),
            pltpu.SemaphoreType.DMA((SPAN, 2, kv_heads)),
            pltpu.SemaphoreType.DMA((kv_heads,)),
            pltpu.SemaphoreType.DMA((kv_heads,)),
            pltpu.SemaphoreType.DMA((3,)),
            pltpu.SemaphoreType.DMA((kv_heads,)),
        ],
        compiler_params=pltpu.CompilerParams(
            collective_id=0, has_side_effects=True, vmem_limit_bytes=56 * 1024 * 1024
        ),
    )(queries, keys, values)


def solution(mesh):
    return jax.shard_map(
        functools.partial(local, mesh.shape["context"]),
        mesh=mesh,
        in_specs=(P(("groups", "context"), "tensor"),) * 3,
        out_specs=P(("groups", "context", "tensor"), None),
        check_vma=False,
    )
```

```python
import functools
import math

import jax
import jax.numpy as jnp
from jax import lax
from jax.experimental import pallas as pl
from jax.experimental.pallas import tpu as pltpu
from jax.sharding import PartitionSpec as P

HEAD_DIM = 128
WINDOW = 2048
SPAN = 4
MESH = pl.DeviceIdType.MESH

CAP = 50.0
SCORE_FACTOR = 144.0 ** (-0.5) / CAP
EXP_FACTOR = CAP * math.log2(math.e)


def kernel(
    blocks,
    q_hbm,
    k_hbm,
    v_hbm,
    out_ref,
    q_ref,
    k_ref,
    v_ref,
    held,
    acc,
    outgoing,
    kept,
    up_own_send,
    up_relay_send,
    cross_send,
    recv_sem,
    out_send,
    out_recv,
    fetch_sem,
    keep_sem,
):
    rows = q_ref.shape[0]
    half = rows // 2
    kv_heads = k_ref.shape[1] // HEAD_DIM
    own_cols = q_ref.shape[1]
    c = lax.axis_index("context")
    t = lax.axis_index("tensor")
    odd = lax.rem(c, 2)
    pair = c + 1 - 2 * odd
    other = 1 - t
    has_up = c + 2 < blocks
    has_down = c >= 2

    fetches = [
        pltpu.make_async_copy(far, near, fetch_sem.at[at])
        for at, (far, near) in enumerate(((q_hbm, q_ref), (k_hbm, k_ref), (v_hbm, v_ref)))
    ]
    for fetch in fetches:
        fetch.start()

    barrier = pltpu.get_barrier_semaphore()
    pl.semaphore_signal(barrier, inc=1, device_id={"context": pair}, device_id_type=MESH)
    pl.semaphore_signal(barrier, inc=1, device_id={"tensor": other}, device_id_type=MESH)

    @pl.when(has_up)
    def _():
        pl.semaphore_signal(barrier, inc=1, device_id={"context": c + 2}, device_id_type=MESH)

    @pl.when(has_down)
    def _():
        pl.semaphore_signal(barrier, inc=1, device_id={"context": c - 2}, device_id_type=MESH)

    pl.semaphore_wait(barrier, 2 + has_up.astype(jnp.int32) + has_down.astype(jnp.int32))

    def columns(head):
        return pl.ds(pl.multiple_of(head * HEAD_DIM, HEAD_DIM), HEAD_DIM)

    def source(slot, which, h):
        if slot == 0:
            return (k_ref, v_ref)[which].at[:, columns(h)]
        return held.at[slot - 1, which, h]

    def copy(slot, into, which, h, to, send):
        return pltpu.make_async_remote_copy(
            src_ref=(
                (k_hbm, v_hbm)[which].at[:, columns(h)]
                if slot == 0
                else held.at[slot - 1, which, h]
            ),
            dst_ref=held.at[into - 1, which, h],
            send_sem=send,
            recv_sem=recv_sem.at[into - 1, which, h],
            device_id={"context": to},
            device_id_type=MESH,
        )

    def up_own(which, h):
        return copy(0, 2, which, h, c + 2, up_own_send.at[which, h])

    def up_relay(which, h):
        return copy(2, 4, which, h, c + 2, up_relay_send.at[which, h])

    def cross(slot, into, which, h):
        return copy(slot, into, which, h, pair, cross_send.at[(into - 1) // 2, which, h])

    def landed(slot, which, h):
        copy(0, slot, which, h, pair, cross_send.at[0, which, h]).wait_recv()

    def terms(h, g, row_at, row_count, slot, key_at, key_count, mask):
        q = q_ref[pl.ds(row_at, row_count), columns(2 * h + g)]
        key_rows = source(slot, 0, h)[pl.ds(key_at, key_count), :]
        value_rows = source(slot, 1, h)[pl.ds(key_at, key_count), :]
        scores = lax.dot_general(
            q, key_rows, (((1,), (1,)), ((), ())), preferred_element_type=jnp.float32
        )
        exp_terms = jnp.exp2(EXP_FACTOR * jnp.tanh(scores * SCORE_FACTOR))
        if mask is not None:
            i = row_at + lax.broadcasted_iota(jnp.int32, exp_terms.shape, 0)
            j = key_at + lax.broadcasted_iota(jnp.int32, exp_terms.shape, 1)
            allowed = j <= i if mask == "own" else j > i
            exp_terms = jnp.where(allowed, exp_terms, jnp.zeros_like(exp_terms))
        beside = jnp.concatenate([value_rows, jnp.ones_like(value_rows)], axis=1)
        return jnp.dot(
            exp_terms.astype(jnp.bfloat16), beside, preferred_element_type=jnp.float32
        )

    def attend_own(h):
        @pl.loop(0, 2)
        def _(g):
            acc[2 * h + g, pl.ds(0, half), :] = terms(h, g, 0, half, 0, 0, half, "own")
            acc[2 * h + g, pl.ds(half, half), :] = terms(h, g, half, half, 0, 0, rows, "own")

    def attend_far(h):
        @pl.loop(0, 2)
        def _(g):
            acc[2 * h + g, pl.ds(0, half), :] += terms(h, g, 0, half, 4, 0, rows, "far")
            acc[2 * h + g, pl.ds(half, half), :] += terms(h, g, half, half, 4, half, half, "far")

    def attend_whole(h, slot):
        @pl.loop(0, 4)
        def _(step):
            g = step // 2
            row_at = pl.multiple_of(lax.rem(step, 2) * half, half)
            acc[2 * h + g, pl.ds(row_at, half), :] += terms(
                h, g, row_at, half, slot, 0, rows, None
            )

    def send_own(h, which):
        @pl.when(has_up)
        def _():
            up_own(which, h).start()

        @pl.when(odd == 0)
        def _():
            cross(0, 1, which, h).start()

    def sent_own(h, which):
        @pl.when(has_up)
        def _():
            up_own(which, h).wait_send()

        @pl.when(odd == 0)
        def _():
            cross(0, 1, which, h).wait_send()

    def send_relay(h, which):
        @pl.when(has_up & has_down)
        def _():
            up_relay(which, h).start()

        @pl.when((odd == 0) & has_down)
        def _():
            cross(2, 3, which, h).start()

    def sent_relay(h, which):
        @pl.when(has_up & has_down)
        def _():
            up_relay(which, h).wait_send()

        @pl.when((odd == 0) & has_down)
        def _():
            cross(2, 3, which, h).wait_send()

    def take(slot, h, which):
        @pl.when(c >= slot)
        def _():
            landed(slot, which, h)

            @pl.when(odd == 1)
            def _():
                cross(slot, slot - 1, which, h).start()

    def attend(slot, h):
        @pl.when(c >= slot)
        def _():
            if slot % 2 == 1:
                for which in range(2):
                    landed(slot, which, h)
            if slot == 4:
                attend_far(h)
            else:
                attend_whole(h, slot)

    def out_columns(h):
        col = pl.multiple_of(t * own_cols + h * 2 * HEAD_DIM, 2 * HEAD_DIM)
        return out_ref.at[:, pl.ds(col, 2 * HEAD_DIM)]

    def keep(h):
        return pltpu.make_async_copy(kept.at[h], out_columns(h), keep_sem.at[h])

    def hand_over(h):
        return pltpu.make_async_remote_copy(
            src_ref=outgoing.at[h],
            dst_ref=out_columns(h),
            send_sem=out_send.at[h],
            recv_sem=out_recv.at[h],
            device_id={"tensor": other},
            device_id_type=MESH,
        )

    def finish(h):
        attend(3, h)

        def finished(g, owner):
            part = acc[2 * h + g, pl.ds(pl.multiple_of(owner * half, half), half), :]
            return (part[:, :HEAD_DIM] / part[:, HEAD_DIM:]).astype(out_ref.dtype)

        for g in range(2):
            outgoing[h, :, pl.ds(g * HEAD_DIM, HEAD_DIM)] = finished(g, other)
        hand_over(h).start()
        for g in range(2):
            kept[h, :, pl.ds(g * HEAD_DIM, HEAD_DIM)] = finished(g, t)
        keep(h).start()

    last = kv_heads - 1
    for which in range(2):
        send_own(0, which)
    for fetch in fetches:
        fetch.wait()
    attend_own(0)

    @pl.loop(1, kv_heads)
    def _(h):
        sent_own(h - 1, 0)
        send_own(h, 0)
        take(2, h - 1, 0)
        attend_own(h)
        sent_own(h - 1, 1)
        send_own(h, 1)
        take(2, h - 1, 1)
        attend(2, h - 1)

        @pl.when(h >= 2)
        def _():
            attend(1, h - 2)

    for which in range(2):
        sent_own(last, which)
        send_relay(0, which)
        take(2, last, which)
        if which == 0:
            attend(1, last - 1)
    attend(2, last)

    for which in range(2):
        sent_relay(0, which)
        send_relay(1, which)
        take(4, 0, which)
        if which == 0:
            attend(1, last)
    attend(4, 0)

    @pl.loop(2, kv_heads)
    def _(h):
        sent_relay(h - 1, 0)
        send_relay(h, 0)
        take(4, h - 1, 0)
        finish(h - 2)
        sent_relay(h - 1, 1)
        send_relay(h, 1)
        take(4, h - 1, 1)
        attend(4, h - 1)

    for which in range(2):
        take(4, last, which)
    finish(last - 1)
    attend(4, last)
    finish(last)
    for which in range(2):
        sent_relay(last, which)

    @pl.loop(0, kv_heads)
    def _(h):
        keep(h).wait()
        hand_over(h).wait()
        for which in range(2):

            @pl.when((odd == 1) & (c >= 2))
            def _():
                cross(2, 1, which, h).wait_send()

            @pl.when((odd == 1) & (c >= 4))
            def _():
                cross(4, 3, which, h).wait_send()


def local(blocks, queries, keys, values):
    rows = queries.shape[0]
    kv_heads = keys.shape[1] // HEAD_DIM
    heads = queries.shape[1] // HEAD_DIM
    assert WINDOW == SPAN * rows and blocks % 2 == 0 and heads == 2 * kv_heads
    return pl.pallas_call(
        functools.partial(kernel, blocks),
        out_shape=jax.ShapeDtypeStruct((rows // 2, 2 * queries.shape[1]), queries.dtype),
        in_specs=[pl.BlockSpec(memory_space=pltpu.HBM)] * 3,
        out_specs=pl.BlockSpec(memory_space=pltpu.HBM),
        scratch_shapes=[
            pltpu.VMEM(queries.shape, queries.dtype),
            pltpu.VMEM(keys.shape, keys.dtype),
            pltpu.VMEM(values.shape, values.dtype),
            pltpu.VMEM((SPAN, 2, kv_heads, rows, HEAD_DIM), keys.dtype),
            pltpu.VMEM((heads, rows, 2 * HEAD_DIM), jnp.float32),
            pltpu.VMEM((kv_heads, rows // 2, 2 * HEAD_DIM), queries.dtype),
            pltpu.VMEM((kv_heads, rows // 2, 2 * HEAD_DIM), queries.dtype),
            pltpu.SemaphoreType.DMA((2, kv_heads)),
            pltpu.SemaphoreType.DMA((2, kv_heads)),
            pltpu.SemaphoreType.DMA((2, 2, kv_heads)),
            pltpu.SemaphoreType.DMA((SPAN, 2, kv_heads)),
            pltpu.SemaphoreType.DMA((kv_heads,)),
            pltpu.SemaphoreType.DMA((kv_heads,)),
            pltpu.SemaphoreType.DMA((3,)),
            pltpu.SemaphoreType.DMA((kv_heads,)),
        ],
        compiler_params=pltpu.CompilerParams(
            collective_id=0, has_side_effects=True, vmem_limit_bytes=56 * 1024 * 1024
        ),
    )(queries, keys, values)


def solution(mesh):
    return jax.shard_map(
        functools.partial(local, mesh.shape["context"]),
        mesh=mesh,
        in_specs=(P(("groups", "context"), "tensor"),) * 3,
        out_specs=P(("groups", "context", "tensor"), None),
        check_vma=False,
    )
```
